32 devices in a mesh: tm: 8 (over z, x), cam: 4 (over y, core).
Axes of the slice: x: 2, y: 2, z: 4, core: 2. Of those that a mesh axis runs over, the one named last changes fastest.
Arguments:
- tokens: bfloat16 [4, 8, 512, 1536], P('cam', 'tm'), may hold values from -6 to 6
- w_query: bfloat16 [1536, 768], replicated, may hold values from -18 to 18
- w_key: bfloat16 [1536, 768], replicated, may hold values from -1 to 1
- w_value: bfloat16 [1536, 768], replicated, may hold values from -0.15625 to 0.15625
- w_out: bfloat16 [768, 1536], replicated, may hold values from -1.75 to 1.75
- grad_update: bfloat16 [4, 8, 512, 1536], P('cam', 'tm'), may hold values from -6 to 6
- memory_offsets: int32 [8, 4], replicated, may hold values from 1 to 7, as said below
- strip_count: int32 [4, 4], replicated, may hold values from 0 to 2, as said below
- strip_index: int32 [4, 4, 2], replicated, may hold values from 0 to 3, as said below
Outputs:
- update: bfloat16 [4, 8, 512, 1536], P('cam', 'tm')
- grad_tokens: bfloat16 [4, 8, 512, 1536], P('cam', 'tm')
The draws below stay inside these ranges and needn't reach their ends.
Inputs may be any that keep to these rules, and one draw needn't show every extreme that they name: `memory_offsets`: every entry of row f is at most max(f, 1). strip_count[c, c] is 0. For every camera c the sum over s of strip_count[s, c] is at most 4; it is exactly 4 for some camera, and some entry is 2. The 2 entries of strip_index[s, c] are different.
All inputs are finite; a program needn't handle non-finite values.
Results may differ from the reference program's by a relative error of at most 0.0085.
The reference program's roundings to bfloat16 on the way count: a program that leaves them out, or rounds other values in their place, can miss the bound.
Values may be sent and summed in bfloat16 or wider, within the bound.
A program may use at most 128 MiB of HBM per device.

```python
import math
import jax
import jax.numpy as jnp
from jax import lax

D = 1536
HEADS = 12
HDIM = 64
INNER = 768
P_SIZE = 512
STRIP = 128
NSTRIP = 4
MEM = 32
POOL = 16
NOFF = 4
SMAX = 2
RMAX = 4
FRAMES = 8
CAMS = 4


def shared_base(key):
    raw_normal = jax.random.normal(jax.random.fold_in(key, 7), (D, HEADS * HDIM), jnp.float32)
    return jnp.clip(raw_normal, -5.0, 5.0) / math.sqrt(D)


def draw_w_key(key, part):
    return shared_base(key).astype(jnp.bfloat16)


def draw_w_query(key, part):
    fresh_part = jax.random.normal(jax.random.fold_in(key, 11), (D, HEADS * HDIM), jnp.float32)
    fresh_part = jnp.clip(fresh_part, -5.0, 5.0) / math.sqrt(D)
    return fresh_part.astype(jnp.bfloat16)


def draw_tokens(key, part):
    full_shape = (CAMS, FRAMES, P_SIZE, D)
    raw_normal = jax.random.normal(jax.random.fold_in(key, 3), full_shape, jnp.float32)
    return jnp.clip(raw_normal, -6.0, 6.0).astype(jnp.bfloat16)


def draw_memory_offsets(key, part):
    frame_ids = jnp.arange(FRAMES, dtype=jnp.int32)[:, None]
    reach_max = jnp.maximum(frame_ids, 1)
    raw_draw = jax.random.randint(jax.random.fold_in(key, 13), (FRAMES, NOFF), 0, 1 << 20, dtype=jnp.int32)
    offsets = 1 + raw_draw % reach_max
    return offsets.at[FRAMES - 1, 0].set(FRAMES - 1).astype(jnp.int32)


def draw_strip_count(key, part):
    senders = jnp.arange(CAMS, dtype=jnp.int32)
    raw_draw = jax.random.randint(jax.random.fold_in(key, 17), (CAMS, CAMS), 1, SMAX + 1, dtype=jnp.int32)
    off_diagonal = 1 - jnp.eye(CAMS, dtype=jnp.int32)
    wanted = raw_draw * off_diagonal
    capped = jnp.minimum(jnp.cumsum(wanted, axis=0, dtype=jnp.int32), RMAX)
    counts = capped - jnp.concatenate([jnp.zeros((1, CAMS), jnp.int32), capped[:-1]], axis=0)
    busiest = jax.random.randint(jax.random.fold_in(key, 23), (), 0, CAMS, dtype=jnp.int32)
    order_pos = (senders - busiest - 1) % CAMS
    forced = jnp.minimum(SMAX, jnp.maximum(0, RMAX - order_pos * SMAX))
    forced = jnp.where(senders == busiest, 0, forced)
    return jnp.where(senders[None, :] == busiest, forced[:, None], counts).astype(jnp.int32)


def draw_strip_index(key, part):
    raw_draw = jax.random.randint(jax.random.fold_in(key, 29), (CAMS, CAMS, NSTRIP), 0, 1 << 20, dtype=jnp.int32)
    scores_int = raw_draw * NSTRIP + jnp.arange(NSTRIP, dtype=jnp.int32)
    picked = jnp.argsort(scores_int, axis=-1, stable=True)[..., :SMAX].astype(jnp.int32)
    slot_ids = jnp.arange(SMAX, dtype=jnp.int32)
    picked = picked.at[0, 1].set(NSTRIP - 1 - slot_ids)
    picked = picked.at[1, 0].set(slot_ids)
    return picked.astype(jnp.int32)


def steps_of(rng, shape, cuts, least, high):
    def one(axis_at, blocks):
        steps = jax.random.uniform(jax.random.fold_in(jax.random.fold_in(rng, 6), axis_at), (blocks,), jnp.float32, least / len(cuts), high / len(cuts))
        return jnp.repeat(jnp.exp(steps), shape[axis_at] // blocks).reshape((-1,) + (1,) * (len(shape) - axis_at - 1))

    gain = one(*cuts[0])
    for cut in cuts[1:]:
        gain = gain * one(*cut)
    return gain


def noise(stream_key, shape, width, most, shards=(), held_as=jnp.bfloat16):
    drawn = width * jax.random.normal(stream_key, shape, jnp.float32)
    if shards:
        drawn = drawn * steps_of(stream_key, shape, shards, -0.22, 0.18)
    return jnp.clip(drawn, -most, most).astype(held_as)


def setup_inputs(seed: int = 0) -> dict:
    keys = jax.random.split(jax.random.key(seed), 10)
    tokens = draw_tokens(jax.random.fold_in(keys[9], 71), 0)
    w_query = draw_w_query(jax.random.fold_in(keys[9], 71), 0)
    w_key = draw_w_key(jax.random.fold_in(keys[9], 71), 0)
    w_value = noise(keys[3], (D, INNER), D ** -0.5, 0.15625)
    w_out = noise(keys[4], (INNER, D), (max(INNER // 64, 1)) ** -0.5, 1.75)
    grad_update = noise(keys[5], (CAMS, FRAMES, P_SIZE, D), 1.0, 6.0, ((0, 4), (1, 8)))
    memory_offsets = draw_memory_offsets(jax.random.fold_in(keys[9], 71), 0)
    strip_count = draw_strip_count(jax.random.fold_in(keys[9], 71), 0)
    strip_index = draw_strip_index(jax.random.fold_in(keys[9], 71), 0)
    return {"tokens": tokens, "w_query": w_query, "w_key": w_key, "w_value": w_value, "w_out": w_out, "grad_update": grad_update, "memory_offsets": memory_offsets, "strip_count": strip_count, "strip_index": strip_index}


EPS = 1e-05

def normalize(values_in):
    widened = values_in.astype(jnp.float32)
    average = lax.optimization_barrier(jnp.mean(widened, axis=-1, keepdims=True))
    centred = widened - average
    spread = lax.optimization_barrier(jnp.mean(centred * centred, axis=-1, keepdims=True))
    inverse = lax.rsqrt(spread + EPS)
    return (centred * inverse, inverse)

def norm_backward(grad_normed, normed, inverse):
    first_mean = lax.optimization_barrier(jnp.mean(grad_normed, axis=-1, keepdims=True))
    second_mean = lax.optimization_barrier(jnp.mean(grad_normed * normed, axis=-1, keepdims=True))
    return inverse * (grad_normed - first_mean - normed * second_mean)

def head_pass(queries, key_rows, value_rows, key_live, grad_mixed):
    row_count = queries.shape[0]
    key_count = key_rows.shape[0]
    score_scale = 1.0 / math.sqrt(HDIM)
    query_four = queries.astype(jnp.float32).reshape(row_count, HEADS, HDIM)
    key_four = key_rows.astype(jnp.float32).reshape(key_count, HEADS, HDIM)
    value_four = value_rows.astype(jnp.float32).reshape(key_count, HEADS, HDIM)
    grad_four = grad_mixed.astype(jnp.float32).reshape(row_count, HEADS, HDIM)
    scores = jnp.einsum('qhd,khd->hqk', query_four, key_four) * score_scale
    scores = jnp.where(key_live[None, None, :], scores, -jnp.inf)
    highest = lax.optimization_barrier(jnp.max(scores, axis=-1, keepdims=True))
    shifted_exp = jnp.exp(scores - highest)
    weights = shifted_exp / lax.optimization_barrier(jnp.sum(shifted_exp, axis=-1, keepdims=True))
    weights_low = lax.optimization_barrier(weights.astype(jnp.bfloat16)).astype(jnp.float32)
    mixed_rows = jnp.einsum('hqk,khd->qhd', weights_low, value_four)
    mixed_rows = mixed_rows.reshape(row_count, HEADS * HDIM).astype(jnp.bfloat16)
    grad_weights = jnp.einsum('qhd,khd->hqk', grad_four, value_four)
    inner_sum = lax.optimization_barrier(jnp.sum(weights * grad_weights, axis=-1, keepdims=True))
    grad_scores = (weights * (grad_weights - inner_sum) * score_scale).astype(jnp.bfloat16)
    grad_scores = lax.optimization_barrier(grad_scores).astype(jnp.float32)
    grad_query = jnp.einsum('hqk,khd->qhd', grad_scores, key_four)
    grad_query = grad_query.reshape(row_count, HEADS * HDIM).astype(jnp.bfloat16)
    grad_key = jnp.einsum('hqk,qhd->khd', grad_scores, query_four).reshape(key_count, HEADS * HDIM)
    grad_value = jnp.einsum('hqk,qhd->khd', weights_low, grad_four).reshape(key_count, HEADS * HDIM)
    return (mixed_rows, grad_query, grad_key, grad_value)

def gather_back(own_grads, memory_grads, far_grads, source_safe, source_live, strip_count, strip_index):
    own_grid = own_grads.reshape(CAMS, FRAMES, MEM, POOL, INNER)
    memory_grid = memory_grads.reshape(CAMS, FRAMES, NOFF, MEM, INNER)
    memory_grid = memory_grid * source_live[None, :, :, None, None].astype(jnp.float32)
    kept_add = jnp.zeros((CAMS, FRAMES, MEM, INNER), jnp.float32).at[:, source_safe].add(memory_grid)
    own_grid = own_grid.at[:, :, :, 0].add(kept_add)
    far_grid = far_grads.reshape(CAMS, FRAMES, CAMS, SMAX, STRIP, INNER).astype(jnp.float32)
    slot_ids = jnp.arange(SMAX, dtype=jnp.int32)
    far_live = slot_ids[None, None, :] < jnp.transpose(strip_count)[:, :, None]
    far_grid = far_grid * far_live[:, None, :, :, None, None].astype(jnp.float32)
    sender_ids = jnp.arange(CAMS, dtype=jnp.int32)[None, None, :, None]
    frame_ids = jnp.arange(FRAMES, dtype=jnp.int32)[None, :, None, None]
    strip_ids = jnp.transpose(strip_index, (1, 0, 2))[:, None, :, :]
    strip_grid = own_grid.reshape(CAMS, FRAMES, NSTRIP, STRIP, INNER)
    strip_grid = strip_grid.at[sender_ids, frame_ids, strip_ids].add(far_grid)
    return strip_grid.reshape(CAMS, FRAMES, P_SIZE, INNER).astype(jnp.bfloat16)

def reference(tokens, w_query, w_key, w_value, w_out, grad_update, memory_offsets, strip_count, strip_index):
    all_rows = CAMS * FRAMES * P_SIZE
    normed, inverse = normalize(tokens.reshape(all_rows, D))
    normed_low = normed.astype(jnp.bfloat16)

    def project(weight):
        result = jnp.dot(normed_low, weight, preferred_element_type=jnp.float32)
        return result.astype(jnp.bfloat16).reshape(CAMS, FRAMES, P_SIZE, INNER)
    queries = project(w_query)
    keys_all = project(w_key)
    values_all = project(w_value)
    grad_mixed = jnp.dot(grad_update.reshape(all_rows, D), w_out.T, preferred_element_type=jnp.float32)
    grad_mixed = grad_mixed.astype(jnp.bfloat16).reshape(CAMS, FRAMES, P_SIZE, INNER)
    kept_keys = keys_all[:, :, ::POOL]
    kept_values = values_all[:, :, ::POOL]
    frame_ids = jnp.arange(FRAMES, dtype=jnp.int32)
    sources = frame_ids[:, None] - memory_offsets
    source_live = sources >= 0
    source_safe = jnp.maximum(sources, 0).astype(jnp.int32)
    key_strips = keys_all.reshape(CAMS, FRAMES, NSTRIP, STRIP, INNER)
    value_strips = values_all.reshape(CAMS, FRAMES, NSTRIP, STRIP, INNER)
    senders = jnp.arange(CAMS, dtype=jnp.int32)
    slot_ids = jnp.arange(SMAX, dtype=jnp.int32)

    def per_item(item_id):
        camera = item_id // FRAMES
        frame_at = item_id % FRAMES
        picked_frames = source_safe[frame_at]
        memory_keys = kept_keys[camera][picked_frames].reshape(NOFF * MEM, INNER)
        memory_values = kept_values[camera][picked_frames].reshape(NOFF * MEM, INNER)
        memory_live = jnp.repeat(source_live[frame_at], MEM)
        chosen = strip_index[:, camera, :]
        far_keys = key_strips[senders[:, None], frame_at, chosen].reshape(CAMS * SMAX * STRIP, INNER)
        far_values = value_strips[senders[:, None], frame_at, chosen].reshape(CAMS * SMAX * STRIP, INNER)
        far_live = jnp.repeat((slot_ids[None, :] < strip_count[:, camera][:, None]).reshape(-1), STRIP)
        key_rows = jnp.concatenate([keys_all[camera, frame_at], memory_keys, far_keys], axis=0)
        value_rows = jnp.concatenate([values_all[camera, frame_at], memory_values, far_values], axis=0)
        key_live = jnp.concatenate([jnp.ones((P_SIZE,), dtype=bool), memory_live, far_live], axis=0)
        mixed_rows, grad_query, grad_key, grad_value = head_pass(queries[camera, frame_at], key_rows, value_rows, key_live, grad_mixed[camera, frame_at])
        update_rows = jnp.dot(mixed_rows, w_out, preferred_element_type=jnp.float32).astype(jnp.bfloat16)
        split_at = P_SIZE + NOFF * MEM
        return (update_rows, grad_query, grad_key[:P_SIZE], grad_value[:P_SIZE], grad_key[P_SIZE:split_at], grad_value[P_SIZE:split_at], grad_key[split_at:].astype(jnp.bfloat16), grad_value[split_at:].astype(jnp.bfloat16))
    results = lax.map(per_item, jnp.arange(CAMS * FRAMES, dtype=jnp.int32))
    update = results[0].reshape(CAMS, FRAMES, P_SIZE, D)
    grad_query = results[1].reshape(all_rows, INNER)
    total_keys = gather_back(results[2], results[4], results[6], source_safe, source_live, strip_count, strip_index)
    total_values = gather_back(results[3], results[5], results[7], source_safe, source_live, strip_count, strip_index)
    grad_normed = jnp.dot(grad_query, w_query.T, preferred_element_type=jnp.float32)
    grad_normed = grad_normed + jnp.dot(total_keys.reshape(all_rows, INNER), w_key.T, preferred_element_type=jnp.float32)
    grad_normed = grad_normed + jnp.dot(total_values.reshape(all_rows, INNER), w_value.T, preferred_element_type=jnp.float32)
    grad_tokens = norm_backward(grad_normed, normed, inverse).astype(jnp.bfloat16).reshape(CAMS, FRAMES, P_SIZE, D)
    return (update, grad_tokens)
```

```python
import functools
import math

import jax
import jax.numpy as jnp
from jax import lax
from jax.experimental import pallas as pl
from jax.experimental.pallas import tpu as pltpu
from jax.sharding import PartitionSpec as P

HDIM = 64
STRIP = 128
MEM = 32
RMAX = 4
EPS = 1e-05
PAIR = 2 * HDIM
WIDE = 2 * PAIR
QB = 256
DEAD = -1e30
SCALE = 1.0 / math.sqrt(HDIM)
MESH = pl.DeviceIdType.MESH
F32 = jnp.float32
BF16 = jnp.bfloat16


def dot(a, b):
    return jnp.dot(a, b, preferred_element_type=F32)


def dot_nt(a, b):
    return lax.dot_general(a, b, (((1,), (1,)), ((), ())), preferred_element_type=F32)


def kernel(
    T,
    C,
    x_hbm,
    wq_hbm,
    wk_hbm,
    wv_hbm,
    wo_hbm,
    gu_hbm,
    off_ref,
    cnt_ref,
    idx_ref,
    upd_hbm,
    gt_hbm,
    x,
    wq,
    wk,
    wv,
    wo,
    gu,
    xn,
    mean_s,
    inv_s,
    kept_mine,
    kept_all,
    mg_send,
    mg_recv,
    kall,
    vall,
    kt_s,
    vt_s,
    bias_s,
    qs,
    gms,
    mixed,
    dq,
    own,
    dk_s,
    dv_s,
    tot,
    gn,
    s_send,
    s_recv,
    b_send,
    b_recv,
    in_sem,
    out_sem,
    kept_ss,
    kept_rs,
    mg_ss,
    mg_rs,
    s_ss,
    s_rs,
    b_ss,
    b_rs,
):
    rows, width = x.shape
    inner = wq.shape[1]
    pairs = inner // PAIR
    reads = off_ref.shape[1]
    slots = idx_ref.shape[2]
    strips = rows // STRIP
    spacing = rows // MEM
    keys = kall.shape[1]
    mem_at = rows
    far_at = rows + reads * MEM
    me = lax.axis_index("tm")
    cam = lax.axis_index("cam")

    loads = [
        pltpu.make_async_copy(src, dst, in_sem.at[i])
        for i, (src, dst) in enumerate(
            [(x_hbm, x), (wk_hbm, wk), (wv_hbm, wv), (wq_hbm, wq), (gu_hbm, gu), (wo_hbm, wo)]
        )
    ]
    for load in loads:
        load.start()

    barrier = pltpu.get_barrier_semaphore()

    def greet(d, carry):
        pl.semaphore_signal(
            barrier, inc=1, device_id=(lax.rem(me + d, T), cam), device_id_type=MESH
        )
        return carry

    lax.fori_loop(1, T, greet, 0)
    for d in range(1, C):
        pl.semaphore_signal(
            barrier, inc=1, device_id=(me, lax.rem(cam + d, C)), device_id_type=MESH
        )

    def kept_copy(d, at, target):
        return pltpu.make_async_remote_copy(
            src_ref=kept_mine,
            dst_ref=kept_all.at[pl.ds(pl.multiple_of(at * MEM, MEM), MEM)],
            send_sem=kept_ss.at[d],
            recv_sem=kept_rs.at[d],
            device_id=(target, cam),
            device_id_type=MESH,
        )

    def mg_copy(d, at, target):
        return pltpu.make_async_remote_copy(
            src_ref=mg_send.at[pl.ds(pl.multiple_of(target * MEM, MEM), MEM)],
            dst_ref=mg_recv.at[pl.ds(pl.multiple_of(at * MEM, MEM), MEM)],
            send_sem=mg_ss.at[d],
            recv_sem=mg_rs.at[d],
            device_id=(target, cam),
            device_id_type=MESH,
        )

    def strip_copy(p, d):
        return pltpu.make_async_remote_copy(
            src_ref=s_send.at[p, d - 1],
            dst_ref=s_recv.at[p, d - 1],
            send_sem=s_ss.at[p, d - 1],
            recv_sem=s_rs.at[p, d - 1],
            device_id=(me, lax.rem(cam + d, C)),
            device_id_type=MESH,
        )

    def back_copy(p, d):
        return pltpu.make_async_remote_copy(
            src_ref=b_send.at[p, d - 1],
            dst_ref=b_recv.at[p, d - 1],
            send_sem=b_ss.at[p, d - 1],
            recv_sem=b_rs.at[p, d - 1],
            device_id=(me, lax.rem(cam + C - d, C)),
            device_id_type=MESH,
        )

    block = 64
    loads[0].wait()

    def norm_step(i, carry):
        at = pl.ds(pl.multiple_of(i * block, block), block)
        wide = x[at, :].astype(F32)
        average = jnp.mean(wide, axis=-1, keepdims=True)
        centred = wide - average
        spread = jnp.mean(centred * centred, axis=-1, keepdims=True)
        inverse = lax.rsqrt(spread + EPS)
        mean_s[at, :] = average
        inv_s[at, :] = inverse
        xn[at, :] = (centred * inverse).astype(BF16)
        return carry

    lax.fori_loop(0, rows // block, norm_step, 0)

    pick = (
        lax.broadcasted_iota(jnp.int32, (MEM, rows), 1)
        == lax.broadcasted_iota(jnp.int32, (MEM, rows), 0) * spacing
    ).astype(F32).astype(BF16)
    kept_x = dot(pick, xn[...]).astype(BF16)
    loads[1].wait()
    loads[2].wait()
    kept_mine[:, :inner] = dot(kept_x, wk[...]).astype(BF16)
    kept_mine[:, inner:] = dot(kept_x, wv[...]).astype(BF16)
    pl.semaphore_wait(barrier, T - 1 + C - 1)

    def kept_start(d, carry):
        @pl.when(me + d < T)
        def _():
            kept_copy(d, me, me + d).start()

        return carry

    lax.fori_loop(1, T, kept_start, 0)

    def kv_step(i, carry):
        cols = pl.ds(pl.multiple_of(i * WIDE, WIDE), WIDE)
        k = dot(xn[...], wk[:, cols]).astype(BF16)
        v = dot(xn[...], wv[:, cols]).astype(BF16)
        for u in range(2):
            p = 2 * i + u
            kall[p, :rows, :] = k[:, u * PAIR : (u + 1) * PAIR]
            vall[p, :rows, :] = v[:, u * PAIR : (u + 1) * PAIR]
        for u in range(2):
            p = 2 * i + u
            for d in range(1, C):
                for t in range(slots):
                    strip = idx_ref[cam, lax.rem(cam + d, C), t]
                    for kv, full in ((0, kall), (1, vall)):
                        part = full[p, :STRIP, :]
                        for n in range(1, strips):
                            part = jnp.where(strip == n, full[p, n * STRIP : (n + 1) * STRIP, :], part)
                        s_send[p, d - 1, t, kv] = part
                strip_copy(p, d).start()
        return carry

    lax.fori_loop(0, pairs // 2, kv_step, 0)

    loads[3].wait()
    loads[4].wait()
    loads[5].wait()

    def q_step(i, carry):
        cols = pl.ds(pl.multiple_of(i * WIDE, WIDE), WIDE)
        q = dot(xn[...], wq[:, cols]).astype(BF16) * jnp.asarray(SCALE, BF16)
        g = dot_nt(gu[...], wo[cols, :]).astype(BF16)
        for u in range(2):
            p = 2 * i + u
            qs[p] = q[:, u * PAIR : (u + 1) * PAIR]
            gms[p] = g[:, u * PAIR : (u + 1) * PAIR]
        return carry

    lax.fori_loop(0, pairs // 2, q_step, 0)

    sources = [me - off_ref[me, j] for j in range(reads)]
    counts = [cnt_ref[lax.rem(cam + C - d, C), cam] for d in range(1, C)]
    position = []
    before = jnp.int32(0)
    for count in counts:
        for t in range(slots):
            position.append(jnp.where(t < count, before + t, -1))
        before = before + count
    lane = lax.broadcasted_iota(jnp.int32, (1, PAIR), 1)
    for h in range(2):
        other = PAIR // 2 if h == 0 else 0
        bias_s[h] = jnp.zeros((keys, PAIR), BF16)
        for j in range(reads):
            level = jnp.where(sources[j] >= 0, 0.0, DEAD).astype(F32)
            part = jnp.where(
                lax.broadcasted_iota(jnp.int32, (MEM, PAIR), 1) == other, level, 0.0
            )
            bias_s[h, mem_at + j * MEM : mem_at + (j + 1) * MEM, :] = part.astype(BF16)
        for r in range(RMAX):
            level = jnp.where(r < before, 0.0, DEAD).astype(F32)
            part = jnp.where(
                lax.broadcasted_iota(jnp.int32, (STRIP, PAIR), 1) == other, level, 0.0
            )
            bias_s[h, far_at + r * STRIP : far_at + (r + 1) * STRIP, :] = part.astype(BF16)

    def zero_step(t, carry):
        mg_recv[pl.ds(pl.multiple_of(t * MEM, MEM), MEM), :] = jnp.zeros((MEM, 2 * inner), BF16)
        return carry

    lax.fori_loop(0, me + 1, zero_step, 0)

    def kept_end(d, carry):
        @pl.when(me - d >= 0)
        def _():
            kept_copy(d, me - d, me).wait_recv()

        return carry

    lax.fori_loop(1, T, kept_end, 0)
    for p in range(pairs):
        for full in (kall, vall):
            full[p, mem_at:far_at, :] = jnp.zeros((reads * MEM, PAIR), BF16)

    def read_step(g, carry):
        part = kept_all[pl.ds(pl.multiple_of(g * MEM, MEM), MEM), :]
        for j in range(reads):
            hit = sources[j] == g
            at = slice(mem_at + j * MEM, mem_at + (j + 1) * MEM)
            for p in range(pairs):
                for first, full in ((0, kall), (inner, vall)):
                    new = part[:, first + p * PAIR : first + (p + 1) * PAIR]
                    full[p, at, :] = jnp.where(hit, new, full[p, at, :])
        return carry

    lax.fori_loop(0, me, read_step, 0)

    def pair_step(p, carry):
        for d in range(1, C):
            strip_copy(p, d).wait_recv()
        for kv, full in ((0, kall), (1, vall)):
            got = [s_recv[p, d, t, kv] for d in range(C - 1) for t in range(slots)]
            for r in range(RMAX):
                part = got[0]
                for s in range(1, len(got)):
                    part = jnp.where(position[s] == r, got[s], part)
                full[p, far_at + r * STRIP : far_at + (r + 1) * STRIP, :] = part
        k_pair = kall[p]
        v_pair = vall[p]
        kt_s[...] = (k_pair.astype(F32) * SCALE).T.astype(BF16)
        vt_s[...] = v_pair.astype(F32).T.astype(BF16)
        in_head = [lane < HDIM, lane >= HDIM]
        zero = jnp.zeros((), BF16)
        mixed_t = [[None] * (rows // QB) for _ in range(2)]
        dq_t = [[None] * (rows // QB) for _ in range(2)]
        for b in range(rows // QB):
            q_blk = qs[p, b * QB : (b + 1) * QB, :]
            g_blk = gms[p, b * QB : (b + 1) * QB, :]
            for h in range(2):
                one = (lane == (HDIM if h == 0 else 0)).astype(F32).astype(BF16)
                k_h = jnp.where(in_head[h], k_pair, bias_s[h])
                v_h = jnp.where(in_head[h], v_pair, zero)
                q_one = jnp.where(in_head[h], q_blk, one)
                q_h = jnp.where(in_head[h], q_blk, zero)
                g_h = jnp.where(in_head[h], g_blk, zero)
                scores = dot_nt(k_h, q_one)
                highest = jnp.max(scores, axis=0, keepdims=True)
                lifted = jnp.exp(scores - highest)
                total = jnp.sum(lifted, axis=0, keepdims=True)
                weights = lifted * (1.0 / total)
                low = weights.astype(BF16)
                grad_w = dot_nt(v_h, g_blk)
                inner_sum = jnp.sum(weights * grad_w, axis=0, keepdims=True)
                grad_s = (weights * (grad_w - inner_sum)).astype(BF16)
                mixed_t[h][b] = dot(vt_s[h * HDIM : (h + 1) * HDIM, :], low)
                dq_t[h][b] = dot(kt_s[h * HDIM : (h + 1) * HDIM, :], grad_s)
                dv = dot(low, g_h)
                dk = dot(grad_s, q_h)
                if b == 0 and h == 0:
                    dv_s[...] = dv
                    dk_s[...] = dk
                else:
                    dv_s[...] += dv
                    dk_s[...] += dk
            cols = pl.ds(pl.multiple_of(p * PAIR, PAIR), PAIR)
            at = slice(b * QB, (b + 1) * QB)
            mixed[at, cols] = jnp.concatenate([mixed_t[0][b], mixed_t[1][b]], axis=0).T.astype(BF16)
            dq[at, cols] = jnp.concatenate([dq_t[0][b], dq_t[1][b]], axis=0).T.astype(BF16)
        for kv, grads in ((0, dk_s), (1, dv_s)):
            own[kv, p] = grads[:rows, :]
            cols = pl.ds(pl.multiple_of(kv * inner + p * PAIR, PAIR), PAIR)

            def mem_step(g, carry, grads=grads, cols=cols):
                part = jnp.zeros((MEM, PAIR), F32)
                for j in range(reads):
                    read = grads[mem_at + j * MEM : mem_at + (j + 1) * MEM, :]
                    part = part + jnp.where(sources[j] == g, read, 0.0)
                mg_send[pl.ds(pl.multiple_of(g * MEM, MEM), MEM), cols] = part.astype(BF16)
                return carry

            lax.fori_loop(0, T, mem_step, 0)
            far = [
                grads[far_at + r * STRIP : far_at + (r + 1) * STRIP, :].astype(BF16)
                for r in range(RMAX)
            ]
            for s in range((C - 1) * slots):
                part = jnp.zeros((STRIP, PAIR), BF16)
                for r in range(RMAX):
                    part = jnp.where(position[s] == r, far[r], part)
                b_send[p, s // slots, s % slots, kv] = part
        for d in range(1, C):
            back_copy(p, d).start()
        return carry

    lax.fori_loop(0, pairs, pair_step, 0)

    def mg_start(d, carry):
        @pl.when(me - d >= 0)
        def _():
            mg_copy(d, me, me - d).start()

        return carry

    lax.fori_loop(1, T, mg_start, 0)

    def update_step(i, carry):
        cols = pl.ds(pl.multiple_of(i * WIDE, WIDE), WIDE)
        gu[:, cols] = dot(mixed[...], wo[:, cols]).astype(BF16)
        gn[:, cols] = dot_nt(dq[...], wq[cols, :])
        return carry

    lax.fori_loop(0, width // WIDE, update_step, 0)
    update_out = pltpu.make_async_copy(gu, upd_hbm, out_sem.at[0])
    update_out.start()

    def mg_end(d, carry):
        @pl.when(me + d < T)
        def _():
            mg_copy(d, me + d, me).wait_recv()

        return carry

    lax.fori_loop(1, T, mg_end, 0)
    place = (
        lax.broadcasted_iota(jnp.int32, (rows, T * MEM), 0)
        == lax.rem(lax.broadcasted_iota(jnp.int32, (rows, T * MEM), 1), MEM) * spacing
    ).astype(F32).astype(BF16)

    def total_step(p, carry):
        for d in range(1, C):
            back_copy(p, d).wait_recv()
        for kv in range(2):
            cols = pl.ds(pl.multiple_of(kv * inner + p * PAIR, PAIR), PAIR)
            grown = own[kv, p] + dot(place, mg_recv[:, cols])
            for n in range(strips):
                part = grown[n * STRIP : (n + 1) * STRIP, :]
                for d in range(1, C):
                    came = jnp.zeros((STRIP, PAIR), BF16)
                    for t in range(slots):
                        hit = idx_ref[cam, lax.rem(cam + d, C), t] == n
                        came = jnp.where(hit, b_recv[p, d - 1, t, kv], came)
                    part = part + came.astype(F32)
                tot[n * STRIP : (n + 1) * STRIP, cols] = part.astype(BF16)
        return carry

    lax.fori_loop(0, pairs, total_step, 0)

    def grad_step(i, carry):
        cols = pl.ds(pl.multiple_of(i * WIDE, WIDE), WIDE)
        gn[:, cols] += dot_nt(tot[:, :inner], wk[cols, :]) + dot_nt(tot[:, inner:], wv[cols, :])
        return carry

    lax.fori_loop(0, width // WIDE, grad_step, 0)

    def back_norm_step(i, carry):
        at = pl.ds(pl.multiple_of(i * block, block), block)
        inverse = inv_s[at, :]
        normed = (x[at, :].astype(F32) - mean_s[at, :]) * inverse
        grads = gn[at, :]
        first = jnp.mean(grads, axis=-1, keepdims=True)
        second = jnp.mean(grads * normed, axis=-1, keepdims=True)
        xn[at, :] = (inverse * (grads - first - normed * second)).astype(BF16)
        return carry

    lax.fori_loop(0, rows // block, back_norm_step, 0)
    grad_out = pltpu.make_async_copy(xn, gt_hbm, out_sem.at[1])
    grad_out.start()

    def sent_step(d, carry):
        @pl.when(me + d < T)
        def _():
            kept_copy(d, me, me + d).wait_send()

        @pl.when(me - d >= 0)
        def _():
            mg_copy(d, me, me - d).wait_send()

        return carry

    lax.fori_loop(1, T, sent_step, 0)

    def sent_strip_step(p, carry):
        for d in range(1, C):
            strip_copy(p, d).wait_send()
            back_copy(p, d).wait_send()
        return carry

    lax.fori_loop(0, pairs, sent_strip_step, 0)
    update_out.wait()
    grad_out.wait()


def local(
    T,
    C,
    tokens,
    w_query,
    w_key,
    w_value,
    w_out,
    grad_update,
    memory_offsets,
    strip_count,
    strip_index,
):
    rows, width = tokens.shape[2:]
    inner = w_query.shape[1]
    pairs = inner // PAIR
    reads = memory_offsets.shape[1]
    slots = strip_index.shape[2]
    keys = rows + reads * MEM + RMAX * STRIP
    vmem = pltpu.VMEM
    hbm = pl.BlockSpec(memory_space=pl.ANY)
    smem = pl.BlockSpec(memory_space=pltpu.SMEM)
    strip_shape = (pairs, C - 1, slots, 2, STRIP, PAIR)
    dma = pltpu.SemaphoreType.DMA
    update, grad_tokens = pl.pallas_call(
        functools.partial(kernel, T, C),
        out_shape=[jax.ShapeDtypeStruct((rows, width), BF16)] * 2,
        in_specs=[hbm] * 6 + [smem] * 3,
        out_specs=[hbm] * 2,
        scratch_shapes=[
            vmem((rows, width), BF16),
            vmem((width, inner), BF16),
            vmem((width, inner), BF16),
            vmem((width, inner), BF16),
            vmem((inner, width), BF16),
            vmem((rows, width), BF16),
            vmem((rows, width), BF16),
            vmem((rows, 1), F32),
            vmem((rows, 1), F32),
            vmem((MEM, 2 * inner), BF16),
            vmem((T * MEM, 2 * inner), BF16),
            vmem((T * MEM, 2 * inner), BF16),
            vmem((T * MEM, 2 * inner), BF16),
            vmem((pairs, keys, PAIR), BF16),
            vmem((pairs, keys, PAIR), BF16),
            vmem((PAIR, keys), BF16),
            vmem((PAIR, keys), BF16),
            vmem((2, keys, PAIR), BF16),
            vmem((pairs, rows, PAIR), BF16),
            vmem((pairs, rows, PAIR), BF16),
            vmem((rows, inner), BF16),
            vmem((rows, inner), BF16),
            vmem((2, pairs, rows, PAIR), F32),
            vmem((keys, PAIR), F32),
            vmem((keys, PAIR), F32),
            vmem((rows, 2 * inner), BF16),
            vmem((rows, width), F32),
            vmem(strip_shape, BF16),
            vmem(strip_shape, BF16),
            vmem(strip_shape, BF16),
            vmem(strip_shape, BF16),
            dma((6,)),
            dma((2,)),
            dma((T,)),
            dma((T,)),
            dma((T,)),
            dma((T,)),
            dma((pairs, C - 1)),
            dma((pairs, C - 1)),
            dma((pairs, C - 1)),
            dma((pairs, C - 1)),
        ],
        compiler_params=pltpu.CompilerParams(
            collective_id=0, has_side_effects=True, vmem_limit_bytes=60 * 1024 * 1024
        ),
    )(
        tokens.reshape(rows, width),
        w_query,
        w_key,
        w_value,
        w_out,
        grad_update.reshape(rows, width),
        memory_offsets,
        strip_count,
        strip_index,
    )
    return update.reshape(1, 1, rows, width), grad_tokens.reshape(1, 1, rows, width)


def solution(mesh):
    split = P("cam", "tm", None, None)
    in_specs = (split, P(), P(), P(), P(), split, P(), P(), P())
    return jax.shard_map(
        functools.partial(local, mesh.shape["tm"], mesh.shape["cam"]),
        mesh=mesh,
        in_specs=in_specs,
        out_specs=(split, split),
        check_vma=False,
    )
```

```python
import functools
import math

import jax
import jax.numpy as jnp
from jax import lax
from jax.experimental import pallas as pl
from jax.experimental.pallas import tpu as pltpu
from jax.sharding import PartitionSpec as P

HDIM = 64
STRIP = 128
MEM = 32
RMAX = 4
EPS = 1e-05
PAIR = 2 * HDIM
WIDE = 2 * PAIR
QB = 256
DEAD = -1e30
SCALE = 1.0 / math.sqrt(HDIM)
MESH = pl.DeviceIdType.MESH
F32 = jnp.float32
BF16 = jnp.bfloat16


def dot(a, b):
    return jnp.dot(a, b, preferred_element_type=F32)


def dot_nt(a, b):
    return lax.dot_general(a, b, (((1,), (1,)), ((), ())), preferred_element_type=F32)


def kernel(
    T,
    C,
    x_hbm,
    wq_hbm,
    wk_hbm,
    wv_hbm,
    wo_hbm,
    gu_hbm,
    off_ref,
    cnt_ref,
    idx_ref,
    upd_hbm,
    gt_hbm,
    x,
    wq,
    wk,
    wv,
    wo,
    gu,
    xn,
    mean_s,
    inv_s,
    kept_mine,
    kept_all,
    mg_send,
    mg_recv,
    kall,
    vall,
    kt_s,
    vt_s,
    bias_s,
    qs,
    gms,
    mixed,
    dq,
    own,
    dk_s,
    dv_s,
    tot,
    gn,
    s_send,
    s_recv,
    b_send,
    b_recv,
    in_sem,
    out_sem,
    kept_ss,
    kept_rs,
    mg_ss,
    mg_rs,
    s_ss,
    s_rs,
    b_ss,
    b_rs,
):
    rows, width = x.shape
    inner = wq.shape[1]
    pairs = inner // PAIR
    groups = pairs // 2
    reads = off_ref.shape[1]
    slots = idx_ref.shape[2]
    strips = rows // STRIP
    spacing = rows // MEM
    keys = kall.shape[1]
    mem_at = rows
    far_at = rows + reads * MEM
    me = lax.axis_index("tm")
    cam = lax.axis_index("cam")

    loads = [
        pltpu.make_async_copy(src, dst, in_sem.at[i])
        for i, (src, dst) in enumerate(
            [(x_hbm, x), (wk_hbm, wk), (wv_hbm, wv), (wq_hbm, wq), (gu_hbm, gu), (wo_hbm, wo)]
        )
    ]
    for load in loads:
        load.start()

    barrier = pltpu.get_barrier_semaphore()

    def greet(d, carry):
        pl.semaphore_signal(
            barrier, inc=1, device_id=(lax.rem(me + d, T), cam), device_id_type=MESH
        )
        return carry

    lax.fori_loop(1, T, greet, 0)
    for d in range(1, C):
        pl.semaphore_signal(
            barrier, inc=1, device_id=(me, lax.rem(cam + d, C)), device_id_type=MESH
        )

    def slab(at):
        return pl.ds(pl.multiple_of(at * MEM, MEM), MEM)

    def kept_copy(i, d, at, target):
        return pltpu.make_async_remote_copy(
            src_ref=kept_mine.at[i],
            dst_ref=kept_all.at[i, slab(at)],
            send_sem=kept_ss.at[i, d],
            recv_sem=kept_rs.at[i, d],
            device_id=(target, cam),
            device_id_type=MESH,
        )

    def mg_copy(i, d, at, target):
        return pltpu.make_async_remote_copy(
            src_ref=mg_send.at[i, slab(target)],
            dst_ref=mg_recv.at[i, slab(at)],
            send_sem=mg_ss.at[i, d],
            recv_sem=mg_rs.at[i, d],
            device_id=(target, cam),
            device_id_type=MESH,
        )

    def strip_copy(p, d):
        return pltpu.make_async_remote_copy(
            src_ref=s_send.at[p, d - 1],
            dst_ref=s_recv.at[p, d - 1],
            send_sem=s_ss.at[p, d - 1],
            recv_sem=s_rs.at[p, d - 1],
            device_id=(me, lax.rem(cam + d, C)),
            device_id_type=MESH,
        )

    def back_copy(p, d):
        return pltpu.make_async_remote_copy(
            src_ref=b_send.at[p, d - 1],
            dst_ref=b_recv.at[p, d - 1],
            send_sem=b_ss.at[p, d - 1],
            recv_sem=b_rs.at[p, d - 1],
            device_id=(me, lax.rem(cam + C - d, C)),
            device_id_type=MESH,
        )

    block = 64
    loads[0].wait()

    def norm_step(i, carry):
        at = pl.ds(pl.multiple_of(i * block, block), block)
        wide = x[at, :].astype(F32)
        average = jnp.mean(wide, axis=-1, keepdims=True)
        centred = wide - average
        spread = jnp.mean(centred * centred, axis=-1, keepdims=True)
        inverse = lax.rsqrt(spread + EPS)
        mean_s[at, :] = average
        inv_s[at, :] = inverse
        xn[at, :] = (centred * inverse).astype(BF16)
        return carry

    lax.fori_loop(0, rows // block, norm_step, 0)

    pick = (
        lax.broadcasted_iota(jnp.int32, (MEM, rows), 1)
        == lax.broadcasted_iota(jnp.int32, (MEM, rows), 0) * spacing
    ).astype(F32).astype(BF16)
    kept_x = dot(pick, xn[...]).astype(BF16)
    loads[1].wait()
    loads[2].wait()
    for first, weight in ((0, wk), (WIDE, wv)):
        kept = dot(kept_x, weight[...]).astype(BF16)
        for i in range(groups):
            kept_mine[i, :, first : first + WIDE] = kept[:, i * WIDE : (i + 1) * WIDE]
    pl.semaphore_wait(barrier, T - 1 + C - 1)

    for i in range(groups):

        def kept_start(d, carry, i=i):
            @pl.when(me + d < T)
            def _():
                kept_copy(i, d, me, me + d).start()

            return carry

        lax.fori_loop(1, T, kept_start, 0)

    def kv_step(i, carry):
        cols = pl.ds(pl.multiple_of(i * WIDE, WIDE), WIDE)
        k = dot(xn[...], wk[:, cols]).astype(BF16)
        v = dot(xn[...], wv[:, cols]).astype(BF16)
        for u in range(2):
            p = 2 * i + u
            kall[p, :rows, :] = k[:, u * PAIR : (u + 1) * PAIR]
            vall[p, :rows, :] = v[:, u * PAIR : (u + 1) * PAIR]
        for u in range(2):
            p = 2 * i + u
            for d in range(1, C):
                for t in range(slots):
                    strip = idx_ref[cam, lax.rem(cam + d, C), t]
                    for kv, full in ((0, kall), (1, vall)):
                        part = full[p, :STRIP, :]
                        for n in range(1, strips):
                            part = jnp.where(strip == n, full[p, n * STRIP : (n + 1) * STRIP, :], part)
                        s_send[p, d - 1, t, kv] = part
                strip_copy(p, d).start()
        return carry

    lax.fori_loop(0, pairs // 2, kv_step, 0)

    loads[3].wait()
    loads[4].wait()
    loads[5].wait()

    def q_step(i, carry):
        cols = pl.ds(pl.multiple_of(i * WIDE, WIDE), WIDE)
        q = dot(xn[...], wq[:, cols]).astype(BF16) * jnp.asarray(SCALE, BF16)
        g = dot_nt(gu[...], wo[cols, :]).astype(BF16)
        for u in range(2):
            p = 2 * i + u
            qs[p] = q[:, u * PAIR : (u + 1) * PAIR]
            gms[p] = g[:, u * PAIR : (u + 1) * PAIR]
        return carry

    lax.fori_loop(0, pairs // 2, q_step, 0)

    sources = [me - off_ref[me, j] for j in range(reads)]
    counts = [cnt_ref[lax.rem(cam + C - d, C), cam] for d in range(1, C)]
    position = []
    before = jnp.int32(0)
    for count in counts:
        for t in range(slots):
            position.append(jnp.where(t < count, before + t, -1))
        before = before + count
    lane = lax.broadcasted_iota(jnp.int32, (1, PAIR), 1)
    for h in range(2):
        other = PAIR // 2 if h == 0 else 0
        bias_s[h] = jnp.zeros((keys, PAIR), BF16)
        for j in range(reads):
            level = jnp.where(sources[j] >= 0, 0.0, DEAD).astype(F32)
            part = jnp.where(
                lax.broadcasted_iota(jnp.int32, (MEM, PAIR), 1) == other, level, 0.0
            )
            bias_s[h, mem_at + j * MEM : mem_at + (j + 1) * MEM, :] = part.astype(BF16)
        for r in range(RMAX):
            level = jnp.where(r < before, 0.0, DEAD).astype(F32)
            part = jnp.where(
                lax.broadcasted_iota(jnp.int32, (STRIP, PAIR), 1) == other, level, 0.0
            )
            bias_s[h, far_at + r * STRIP : far_at + (r + 1) * STRIP, :] = part.astype(BF16)

    def zero_step(t, carry):
        for i in range(groups):
            mg_recv[i, slab(t), :] = jnp.zeros((MEM, 2 * WIDE), BF16)
        return carry

    lax.fori_loop(0, me + 1, zero_step, 0)

    for p in range(pairs):
        for full in (kall, vall):
            full[p, mem_at:far_at, :] = jnp.zeros((reads * MEM, PAIR), BF16)

    def read_group(i):
        def kept_end(d, carry):
            @pl.when(me - d >= 0)
            def _():
                kept_copy(i, d, me - d, me).wait_recv()

            return carry

        lax.fori_loop(1, T, kept_end, 0)

        def read_step(g, carry):
            part = kept_all[i, slab(g), :]
            for j in range(reads):
                hit = sources[j] == g
                at = slice(mem_at + j * MEM, mem_at + (j + 1) * MEM)
                for u in range(2):
                    for first, full in ((0, kall), (WIDE, vall)):
                        new = part[:, first + u * PAIR : first + (u + 1) * PAIR]
                        full[2 * i + u, at, :] = jnp.where(hit, new, full[2 * i + u, at, :])
            return carry

        lax.fori_loop(0, me, read_step, 0)

    def pair_step(p, carry):
        group = lax.div(p, 2)
        half = lax.rem(p, 2)

        @pl.when(half == 0)
        def _():
            read_group(group)

        for d in range(1, C):
            strip_copy(p, d).wait_recv()
        for kv, full in ((0, kall), (1, vall)):
            got = [s_recv[p, d, t, kv] for d in range(C - 1) for t in range(slots)]
            for r in range(RMAX):
                part = got[0]
                for s in range(1, len(got)):
                    part = jnp.where(position[s] == r, got[s], part)
                full[p, far_at + r * STRIP : far_at + (r + 1) * STRIP, :] = part
        k_pair = kall[p]
        v_pair = vall[p]
        kt_s[...] = (k_pair.astype(F32) * SCALE).T.astype(BF16)
        vt_s[...] = v_pair.astype(F32).T.astype(BF16)
        in_head = [lane < HDIM, lane >= HDIM]
        zero = jnp.zeros((), BF16)
        mixed_t = [[None] * (rows // QB) for _ in range(2)]
        dq_t = [[None] * (rows // QB) for _ in range(2)]
        for b in range(rows // QB):
            q_blk = qs[p, b * QB : (b + 1) * QB, :]
            g_blk = gms[p, b * QB : (b + 1) * QB, :]
            for h in range(2):
                one = (lane == (HDIM if h == 0 else 0)).astype(F32).astype(BF16)
                k_h = jnp.where(in_head[h], k_pair, bias_s[h])
                v_h = jnp.where(in_head[h], v_pair, zero)
                q_one = jnp.where(in_head[h], q_blk, one)
                q_h = jnp.where(in_head[h], q_blk, zero)
                g_h = jnp.where(in_head[h], g_blk, zero)
                scores = dot_nt(k_h, q_one)
                highest = jnp.max(scores, axis=0, keepdims=True)
                lifted = jnp.exp(scores - highest)
                total = jnp.sum(lifted, axis=0, keepdims=True)
                weights = lifted * (1.0 / total)
                low = weights.astype(BF16)
                grad_w = dot_nt(v_h, g_blk)
                inner_sum = jnp.sum(weights * grad_w, axis=0, keepdims=True)
                grad_s = (weights * (grad_w - inner_sum)).astype(BF16)
                mixed_t[h][b] = dot(vt_s[h * HDIM : (h + 1) * HDIM, :], low)
                dq_t[h][b] = dot(kt_s[h * HDIM : (h + 1) * HDIM, :], grad_s)
                dv = dot(low, g_h)
                dk = dot(grad_s, q_h)
                if b == 0 and h == 0:
                    dv_s[...] = dv
                    dk_s[...] = dk
                else:
                    dv_s[...] += dv
                    dk_s[...] += dk
            cols = pl.ds(pl.multiple_of(p * PAIR, PAIR), PAIR)
            at = slice(b * QB, (b + 1) * QB)
            mixed[at, cols] = jnp.concatenate([mixed_t[0][b], mixed_t[1][b]], axis=0).T.astype(BF16)
            dq[at, cols] = jnp.concatenate([dq_t[0][b], dq_t[1][b]], axis=0).T.astype(BF16)
        for kv, grads in ((0, dk_s), (1, dv_s)):
            own[kv, p] = grads[:rows, :]
            cols = pl.ds(pl.multiple_of(kv * WIDE + half * PAIR, PAIR), PAIR)

            def mem_step(g, carry, grads=grads, cols=cols):
                part = jnp.zeros((MEM, PAIR), F32)
                for j in range(reads):
                    read = grads[mem_at + j * MEM : mem_at + (j + 1) * MEM, :]
                    part = part + jnp.where(sources[j] == g, read, 0.0)
                mg_send[group, slab(g), cols] = part.astype(BF16)
                return carry

            lax.fori_loop(0, T, mem_step, 0)
            far = [
                grads[far_at + r * STRIP : far_at + (r + 1) * STRIP, :].astype(BF16)
                for r in range(RMAX)
            ]
            for s in range((C - 1) * slots):
                part = jnp.zeros((STRIP, PAIR), BF16)
                for r in range(RMAX):
                    part = jnp.where(position[s] == r, far[r], part)
                b_send[p, s // slots, s % slots, kv] = part
        for d in range(1, C):
            back_copy(p, d).start()

        @pl.when(half == 1)
        def _():
            def mg_start(d, carry):
                @pl.when(me - d >= 0)
                def _():
                    mg_copy(group, d, me, me - d).start()

                return carry

            lax.fori_loop(1, T, mg_start, 0)

        return carry

    lax.fori_loop(0, pairs, pair_step, 0)

    def update_step(i, carry):
        cols = pl.ds(pl.multiple_of(i * WIDE, WIDE), WIDE)
        gu[:, cols] = dot(mixed[...], wo[:, cols]).astype(BF16)
        gn[:, cols] = dot_nt(dq[...], wq[cols, :])
        return carry

    lax.fori_loop(0, width // WIDE, update_step, 0)
    update_out = pltpu.make_async_copy(gu, upd_hbm, out_sem.at[0])
    update_out.start()

    place = (
        lax.broadcasted_iota(jnp.int32, (rows, T * MEM), 0)
        == lax.rem(lax.broadcasted_iota(jnp.int32, (rows, T * MEM), 1), MEM) * spacing
    ).astype(F32).astype(BF16)

    def total_step(p, carry):
        group = lax.div(p, 2)
        half = lax.rem(p, 2)

        @pl.when(half == 0)
        def _():
            def mg_end(d, carry):
                @pl.when(me + d < T)
                def _():
                    mg_copy(group, d, me + d, me).wait_recv()

                return carry

            lax.fori_loop(1, T, mg_end, 0)

        for d in range(1, C):
            back_copy(p, d).wait_recv()
        for kv in range(2):
            cols = pl.ds(pl.multiple_of(kv * inner + p * PAIR, PAIR), PAIR)
            came_at = pl.ds(pl.multiple_of(kv * WIDE + half * PAIR, PAIR), PAIR)
            grown = own[kv, p] + dot(place, mg_recv[group, :, came_at])
            for n in range(strips):
                part = grown[n * STRIP : (n + 1) * STRIP, :]
                for d in range(1, C):
                    came = jnp.zeros((STRIP, PAIR), BF16)
                    for t in range(slots):
                        hit = idx_ref[cam, lax.rem(cam + d, C), t] == n
                        came = jnp.where(hit, b_recv[p, d - 1, t, kv], came)
                    part = part + came.astype(F32)
                tot[n * STRIP : (n + 1) * STRIP, cols] = part.astype(BF16)
        return carry

    lax.fori_loop(0, pairs, total_step, 0)

    def grad_step(i, carry):
        cols = pl.ds(pl.multiple_of(i * WIDE, WIDE), WIDE)
        gn[:, cols] += dot_nt(tot[:, :inner], wk[cols, :]) + dot_nt(tot[:, inner:], wv[cols, :])
        return carry

    lax.fori_loop(0, width // WIDE, grad_step, 0)

    def back_norm_step(i, carry):
        at = pl.ds(pl.multiple_of(i * block, block), block)
        inverse = inv_s[at, :]
        normed = (x[at, :].astype(F32) - mean_s[at, :]) * inverse
        grads = gn[at, :]
        first = jnp.mean(grads, axis=-1, keepdims=True)
        second = jnp.mean(grads * normed, axis=-1, keepdims=True)
        xn[at, :] = (inverse * (grads - first - normed * second)).astype(BF16)
        return carry

    lax.fori_loop(0, rows // block, back_norm_step, 0)
    grad_out = pltpu.make_async_copy(xn, gt_hbm, out_sem.at[1])
    grad_out.start()

    def sent_step(d, carry):
        @pl.when(me + d < T)
        def _():
            for i in range(groups):
                kept_copy(i, d, me, me + d).wait_send()

        @pl.when(me - d >= 0)
        def _():
            for i in range(groups):
                mg_copy(i, d, me, me - d).wait_send()

        return carry

    lax.fori_loop(1, T, sent_step, 0)

    def sent_strip_step(p, carry):
        for d in range(1, C):
            strip_copy(p, d).wait_send()
            back_copy(p, d).wait_send()
        return carry

    lax.fori_loop(0, pairs, sent_strip_step, 0)
    update_out.wait()
    grad_out.wait()


def local(
    T,
    C,
    tokens,
    w_query,
    w_key,
    w_value,
    w_out,
    grad_update,
    memory_offsets,
    strip_count,
    strip_index,
):
    rows, width = tokens.shape[2:]
    inner = w_query.shape[1]
    pairs = inner // PAIR
    reads = memory_offsets.shape[1]
    slots = strip_index.shape[2]
    keys = rows + reads * MEM + RMAX * STRIP
    vmem = pltpu.VMEM
    hbm = pl.BlockSpec(memory_space=pl.ANY)
    smem = pl.BlockSpec(memory_space=pltpu.SMEM)
    strip_shape = (pairs, C - 1, slots, 2, STRIP, PAIR)
    dma = pltpu.SemaphoreType.DMA
    update, grad_tokens = pl.pallas_call(
        functools.partial(kernel, T, C),
        out_shape=[jax.ShapeDtypeStruct((rows, width), BF16)] * 2,
        in_specs=[hbm] * 6 + [smem] * 3,
        out_specs=[hbm] * 2,
        scratch_shapes=[
            vmem((rows, width), BF16),
            vmem((width, inner), BF16),
            vmem((width, inner), BF16),
            vmem((width, inner), BF16),
            vmem((inner, width), BF16),
            vmem((rows, width), BF16),
            vmem((rows, width), BF16),
            vmem((rows, 1), F32),
            vmem((rows, 1), F32),
            vmem((pairs // 2, MEM, 2 * WIDE), BF16),
            vmem((pairs // 2, T * MEM, 2 * WIDE), BF16),
            vmem((pairs // 2, T * MEM, 2 * WIDE), BF16),
            vmem((pairs // 2, T * MEM, 2 * WIDE), BF16),
            vmem((pairs, keys, PAIR), BF16),
            vmem((pairs, keys, PAIR), BF16),
            vmem((PAIR, keys), BF16),
            vmem((PAIR, keys), BF16),
            vmem((2, keys, PAIR), BF16),
            vmem((pairs, rows, PAIR), BF16),
            vmem((pairs, rows, PAIR), BF16),
            vmem((rows, inner), BF16),
            vmem((rows, inner), BF16),
            vmem((2, pairs, rows, PAIR), F32),
            vmem((keys, PAIR), F32),
            vmem((keys, PAIR), F32),
            vmem((rows, 2 * inner), BF16),
            vmem((rows, width), F32),
            vmem(strip_shape, BF16),
            vmem(strip_shape, BF16),
            vmem(strip_shape, BF16),
            vmem(strip_shape, BF16),
            dma((6,)),
            dma((2,)),
            dma((pairs // 2, T)),
            dma((pairs // 2, T)),
            dma((pairs // 2, T)),
            dma((pairs // 2, T)),
            dma((pairs, C - 1)),
            dma((pairs, C - 1)),
            dma((pairs, C - 1)),
            dma((pairs, C - 1)),
        ],
        compiler_params=pltpu.CompilerParams(
            collective_id=0, has_side_effects=True, vmem_limit_bytes=60 * 1024 * 1024
        ),
    )(
        tokens.reshape(rows, width),
        w_query,
        w_key,
        w_value,
        w_out,
        grad_update.reshape(rows, width),
        memory_offsets,
        strip_count,
        strip_index,
    )
    return update.reshape(1, 1, rows, width), grad_tokens.reshape(1, 1, rows, width)


def solution(mesh):
    split = P("cam", "tm", None, None)
    in_specs = (split, P(), P(), P(), P(), split, P(), P(), P())
    return jax.shard_map(
        functools.partial(local, mesh.shape["tm"], mesh.shape["cam"]),
        mesh=mesh,
        in_specs=in_specs,
        out_specs=(split, split),
        check_vma=False,
    )
```
